32 devices in a mesh: row: 8 (over z, x), col: 4 (over y, core).
Axes of the slice: x: 2, y: 2, z: 4, core: 2. Of those that a mesh axis runs over, the one named last changes fastest.
Arguments:
- cov: float32 [16384, 16384], P('row', 'col'), as said below
- noise: float32 [16384, 16384], P('row', 'col'), as said below
- diffusivity: float32 [128, 128], P('row'), may hold values from 0.25 to 1
- wind_x: float32 [128, 128], P('row'), may hold values from -1 to 1
- wind_y: float32 [128, 128], P('row'), may hold values from -1 to 1
Outputs:
- cov_next: float32 [16384, 16384], P('row', 'col')
The draws below stay inside these ranges and needn't reach their ends.
Inputs may be any that keep to these rules, and one draw needn't show every extreme that they name: cov is symmetric. noise is symmetric.
All inputs are finite; a program needn't handle non-finite values.
Results may differ from the reference program's by a relative error of at most 0.00002.
Values sent between devices are 32-bit elements; how exact they have to be, the bound alone decides.
A program may use at most 384 MiB of HBM per device.

```python
import math
import jax
import jax.numpy as jnp

G = 128
STATES = 16384


def draw_cov(key, part):
    base = jax.random.normal(key, (STATES, STATES), jnp.float32)
    return 0.5 * (base + base.T) + 3.0 * jnp.eye(STATES, dtype=jnp.float32)


def draw_noise(key, part):
    base = 2.0 * jax.random.normal(key, (STATES, STATES), jnp.float32)
    return 0.5 * (base + base.T) + jnp.eye(STATES, dtype=jnp.float32)


def levels(rng, shape, cuts, least, largest):
    def one(dim, shards_of):
        steps = jax.random.uniform(jax.random.fold_in(jax.random.fold_in(rng, 6), dim), (shards_of,), jnp.float32, least / len(cuts), largest / len(cuts))
        return jnp.repeat(jnp.exp(steps), shape[dim] // shards_of).reshape((-1,) + (1,) * (len(shape) - dim - 1))

    loudness = one(*cuts[0])
    for cut in cuts[1:]:
        loudness = loudness * one(*cut)
    return loudness


def setup_inputs(seed: int = 0) -> dict:
    key_of = jax.random.split(jax.random.key(seed), 6)
    cov = draw_cov(jax.random.fold_in(key_of[5], 71), 0)
    noise = draw_noise(jax.random.fold_in(key_of[5], 71), 0)
    diffusivity = jnp.clip(jnp.exp(math.log(1.0) - 1.3862944 * jax.random.uniform(key_of[2], (G, G), jnp.float32) ** levels(key_of[2], (G, G), ((0, 8),), -0.2, 0.2)), 0.25, 1.0)
    wind_x = jnp.clip(jax.random.uniform(key_of[3], (G, G), jnp.float32, -1.0, 1.0) * levels(key_of[3], (G, G), ((0, 8),), -0.4, 0.0), -1.0, 1.0)
    wind_y = jnp.clip(jax.random.uniform(key_of[4], (G, G), jnp.float32, -1.0, 1.0) * levels(key_of[4], (G, G), ((0, 8),), -0.4, 0.0), -1.0, 1.0)
    return {"cov": cov, "noise": noise, "diffusivity": diffusivity, "wind_x": wind_x, "wind_y": wind_y}


OFFSETS = ((0, 0), (1, 0), (-1, 0), (0, 1), (0, -1), (1, 1), (1, -1), (-1, 1), (-1, -1))
time_step = 0.1


def stencil_weights(kappa, flow_x, flow_y):
    edge = (4.0 / 6.0) * kappa
    corner = kappa / 6.0
    return jnp.stack([(-20.0 / 6.0) * kappa, edge - 0.5 * flow_x, edge + 0.5 * flow_x,
                      edge - 0.5 * flow_y, edge + 0.5 * flow_y, corner, corner, corner, corner])


def row_term(padded, weights):
    count = weights.shape[1]
    side = weights.shape[2]
    wide = jnp.pad(padded, ((0, 0), (1, 1), (0, 0)))
    total = jnp.zeros((count, side, padded.shape[2]), jnp.float32)
    for index, (step_x, step_y) in enumerate(OFFSETS):
        piece = wide[1 + step_x:1 + step_x + count, 1 + step_y:1 + step_y + side, :]
        total = total + weights[index][:, :, None] * piece
    return total


def col_term(padded, weights):
    count = weights.shape[1]
    side = weights.shape[2]
    wide = jnp.pad(padded, ((0, 0), (0, 0), (1, 1)))
    total = jnp.zeros((padded.shape[0], count, side), jnp.float32)
    for index, (step_x, step_y) in enumerate(OFFSETS):
        piece = wide[:, 1 + step_x:1 + step_x + count, 1 + step_y:1 + step_y + side]
        total = total + weights[index][None, :, :] * piece
    return total


def derive(field, noise, weights):
    states = field.shape[0]
    along_rows = row_term(jnp.pad(field.reshape(G, G, states), ((1, 1), (0, 0), (0, 0))), weights)
    along_cols = col_term(jnp.pad(field.reshape(states, G, G), ((0, 0), (1, 1), (0, 0))), weights)
    return along_rows.reshape(states, states) + along_cols.reshape(states, states) + noise


def reference(cov, noise, diffusivity, wind_x, wind_y):
    weights = stencil_weights(diffusivity, wind_x, wind_y)
    first = derive(cov, noise, weights)
    middle = cov + time_step * first
    second = derive(middle, noise, weights)
    return cov + (0.5 * time_step) * (first + second)
```

```python
import functools
import jax
import jax.numpy as jnp
from jax import lax
from jax.experimental import pallas as pl
from jax.experimental.pallas import tpu as pltpu
from jax.sharding import PartitionSpec as P

time_step = 0.1
BOTH = ("row", "col")
BAND = 2


def term_weights(kappa, flow_x, flow_y):
    a = kappa / 6.0
    b = 0.5 * flow_y
    c = 0.5 * flow_x

    def later(v):
        return jnp.pad(v[:, 1:], ((0, 0), (0, 1)))

    def earlier(v):
        return jnp.pad(v[:, :-1], ((0, 0), (1, 0)))

    return jnp.stack(
        [later(a), later(4.0 * a + b), earlier(a), earlier(4.0 * a - b), 4.0 * a + c, 4.0 * a - c, -20.0 * a]
    )


def stencil_kernel(side, scale, up_ref, x_ref, dn_ref, base_ref, rw_ref, cw_ref, o_ref):
    step = pl.program_id(0)
    has_up = (step > 0).astype(jnp.float32)
    has_dn = (step < pl.num_programs(0) - 1).astype(jnp.float32)
    band = x_ref.shape[0] // side
    blocks = x_ref.shape[1] // side

    def block(j, first, last):
        here = pl.ds(pl.multiple_of(j * side, side), side)
        cw = [cw_ref[m : m + 1, here] for m in range(7)]
        for x in range(band):
            rows = slice(x * side, (x + 1) * side)
            rw = [rw_ref[m, rows, :] for m in range(7)]
            mid = x_ref[rows, here]
            up = up_ref[:, here] * has_up if x == 0 else x_ref[(x - 1) * side : x * side, here]
            dn = dn_ref[:, here] * has_dn if x == band - 1 else x_ref[(x + 1) * side : (x + 2) * side, here]
            both = up + dn
            acc = pltpu.roll(rw[0] * both + rw[1] * mid, 1, 0)
            acc = acc + pltpu.roll(rw[2] * both + rw[3] * mid, side - 1, 0)
            acc = acc + (rw[4] * up + rw[5] * dn)
            acc = acc + (rw[6] + cw[6]) * mid
            if scale:
                acc = acc + (base_ref[rows, here] + scale * mid)
            else:
                acc = acc + base_ref[rows, here]
            if not first:
                left = x_ref[rows, pl.ds(pl.multiple_of((j - 1) * side, side), side)]
            if not last:
                right = x_ref[rows, pl.ds(pl.multiple_of((j + 1) * side, side), side)]
            if first:
                both = right
                acc = acc + cw[5] * right
            elif last:
                both = left
                acc = acc + cw[4] * left
            else:
                both = left + right
                acc = acc + (cw[4] * left + cw[5] * right)
            acc = acc + pltpu.roll(cw[0] * both + cw[1] * mid, 1, 1)
            acc = acc + pltpu.roll(cw[2] * both + cw[3] * mid, side - 1, 1)
            o_ref[rows, here] = acc

    block(0, True, False)

    @pl.loop(1, blocks - 1)
    def _(j):
        block(j, False, False)

    block(blocks - 1, False, True)


def local_stencil(field, base, row_w, col_w, side, scale):
    rows, cols = field.shape
    steps = rows // (BAND * side)
    lines = rows // side
    tall = (BAND * side, cols)
    return pl.pallas_call(
        functools.partial(stencil_kernel, side, scale),
        grid=(steps,),
        out_shape=jax.ShapeDtypeStruct((rows, cols), jnp.float32),
        in_specs=[
            pl.BlockSpec((side, cols), lambda i: (jnp.maximum(i * BAND - 1, 0), 0)),
            pl.BlockSpec(tall, lambda i: (i, 0)),
            pl.BlockSpec((side, cols), lambda i: (jnp.minimum(i * BAND + BAND, lines - 1), 0)),
            pl.BlockSpec(tall, lambda i: (i, 0)),
            pl.BlockSpec((7, BAND * side, side), lambda i: (0, i, 0)),
            pl.BlockSpec((8, cols), lambda i: (0, 0)),
        ],
        out_specs=pl.BlockSpec(tall, lambda i: (i, 0)),
        compiler_params=pltpu.CompilerParams(
            dimension_semantics=("arbitrary",), vmem_limit_bytes=50 * 1024 * 1024
        ),
        cost_estimate=pl.CostEstimate(
            flops=34 * rows * cols, bytes_accessed=16 * rows * cols, transcendentals=0
        ),
    )(field, field, field, base, row_w, col_w)


def column_weights(cells, row_axis, col_axis):
    nrow, ncol = lax.axis_size(row_axis), lax.axis_size(col_axis)
    if nrow % ncol:
        every = lax.all_gather(cells, row_axis, axis=1, tiled=True)
        count = every.shape[1] // ncol
        return lax.dynamic_slice_in_dim(every, lax.axis_index(col_axis) * count, count, 1)
    ratio = nrow // ncol
    turn = lax.axis_index(row_axis) // ncol
    parts = []
    for e in range(ratio):
        mine = None
        for f in range(ratio):
            perm = [
                ((ratio * c + e) * ncol + d, (f * ncol + d) * ncol + c) for c in range(ncol) for d in range(ncol)
            ]
            got = lax.ppermute(cells, BOTH, perm)
            mine = got if mine is None else mine + got
        parts.append(mine)
    return jnp.concatenate(parts, axis=1)


def row_halos(field, side):
    nrow, ncol = lax.axis_size("row"), lax.axis_size("col")
    rows, cols = field.shape
    ends = nrow - 1
    if nrow != 2 * ncol:
        above = lax.ppermute(field[rows - side :], "row", [(i, i + 1) for i in range(ends)])
        below = lax.ppermute(field[:side], "row", [(i + 1, i) for i in range(ends)])
        return above, below
    half = cols // 2
    parity = lax.axis_index("row") % 2
    odd = parity == 1
    start = parity * half
    lines = rows // side

    def flat(r, c):
        return r * ncol + c

    def slab(at_even, at_odd):
        at = jnp.where(odd, at_odd * side, at_even * side)
        return lax.dynamic_slice(field, (0, at), (rows, side)).T

    turned_above = lax.ppermute(
        slab(2 * lines - 1, lines - 1),
        BOTH,
        [(flat(2 * c + r % 2, (r - 1) // 2), flat(r, c)) for r in range(1, nrow) for c in range(ncol)],
    )
    turned_below = lax.ppermute(
        slab(lines, 0),
        BOTH,
        [(flat(2 * c + r % 2, (r + 1) // 2), flat(r, c)) for r in range(ends) for c in range(ncol)],
    )
    above = lax.ppermute(
        lax.dynamic_slice(field, (rows - side, start), (side, half)), "row", [(i, i + 1) for i in range(ends)]
    )
    below = lax.ppermute(
        lax.dynamic_slice(field, (0, start), (side, half)), "row", [(i + 1, i) for i in range(ends)]
    )

    def joined(turned, plain):
        return jnp.concatenate([jnp.where(odd, plain, turned), jnp.where(odd, turned, plain)], axis=1)

    return joined(turned_above, above), joined(turned_below, below)


def col_halos(field, side):
    ends = lax.axis_size("col") - 1
    cols = field.shape[1]
    left = lax.ppermute(field[:, cols - side :], "col", [(i, i + 1) for i in range(ends)])
    right = lax.ppermute(field[:, :side], "col", [(i + 1, i) for i in range(ends)])
    return left, right


def corrected(total, halos, row_w, col_w, side):
    (above, below), (left, right) = halos
    rows, cols = total.shape

    def down(v):
        return jnp.pad(v[:-1], ((1, 0), (0, 0)))

    def up(v):
        return jnp.pad(v[1:], ((0, 1), (0, 0)))

    def lanes_on(v):
        return jnp.pad(v[:, :-1], ((0, 0), (1, 0)))

    def lanes_back(v):
        return jnp.pad(v[:, 1:], ((0, 0), (0, 1)))

    def of_row(halo, line, centre):
        w = [row_w[m, line][:, None] for m in range(7)]
        return down(w[0] * halo) + up(w[2] * halo) + w[centre] * halo

    def of_col(halo, line, centre):
        w = [col_w[m, line][None, :] for m in range(7)]
        return lanes_on(w[0] * halo) + lanes_back(w[2] * halo) + w[centre] * halo

    def added(total, piece, at):
        old = lax.slice(total, at, (at[0] + piece.shape[0], at[1] + piece.shape[1]))
        return lax.dynamic_update_slice(total, old + piece, at)

    total = added(total, of_col(left, 0, 4), (0, 0))
    total = added(total, of_col(right, -1, 5), (0, cols - side))
    total = added(total, of_row(above, 0, 4), (0, 0))
    return added(total, of_row(below, -1, 5), (rows - side, 0))


def per_device(cov, noise, diffusivity, wind_x, wind_y):
    side = diffusivity.shape[1]
    rows, cols = cov.shape
    cells = jnp.stack([diffusivity, wind_x, wind_y])
    row_w = term_weights(*cells)
    col_w = term_weights(*column_weights(cells, "row", "col"))

    def kernel_weights(scale):
        wide = jnp.broadcast_to((scale * row_w).reshape(7, rows, 1), (7, rows, side))
        return wide, jnp.pad((scale * col_w).reshape(7, cols), ((0, 1), (0, 0)))

    halos = row_halos(cov, side), col_halos(cov, side)
    first = local_stencil(cov, noise, *kernel_weights(1.0), side, None)
    first = corrected(first, halos, row_w, col_w, side)
    halos = row_halos(first, side), col_halos(first, side)
    scale = 0.5 * time_step * time_step
    out = local_stencil(first, cov, *kernel_weights(scale), side, time_step)
    return corrected(out, halos, scale * row_w, scale * col_w, side)


def solution(mesh):
    return jax.shard_map(
        per_device,
        mesh=mesh,
        in_specs=(P("row", "col"), P("row", "col"), P("row", None), P("row", None), P("row", None)),
        out_specs=P("row", "col"),
        check_vma=False,
    )
```

```python
import functools
import jax
import jax.numpy as jnp
from jax import lax
from jax.experimental import pallas as pl
from jax.experimental.pallas import tpu as pltpu
from jax.sharding import PartitionSpec as P

time_step = 0.1
BOTH = ("row", "col")
second_scale = 0.5 * time_step * time_step
BAND = 2


def term_weights(kappa, flow_x, flow_y):
    a = kappa / 6.0
    b = 0.5 * flow_y
    c = 0.5 * flow_x

    def later(v):
        return jnp.pad(v[:, 1:], ((0, 0), (0, 1)))

    def earlier(v):
        return jnp.pad(v[:, :-1], ((0, 0), (1, 0)))

    return jnp.stack(
        [later(a), later(4.0 * a + b), earlier(a), earlier(4.0 * a - b), 4.0 * a + c, 4.0 * a - c, -20.0 * a]
    )


def stencil_kernel(side, first_stage, x_ref, dn_ref, base_ref, rw_ref, cw_ref, o_ref, carry):
    step = pl.program_id(0)
    has_dn = (step < pl.num_programs(0) - 1).astype(jnp.float32)
    band = x_ref.shape[0] // side
    blocks = x_ref.shape[1] // side

    @pl.when(step == 0)
    def _():
        carry[...] = jnp.zeros_like(carry)

    def block(j, first, last):
        here = pl.ds(pl.multiple_of(j * side, side), side)
        cw = [cw_ref[m : m + 1, here] for m in range(7)]
        for x in range(band):
            rows = slice(x * side, (x + 1) * side)
            rw = [rw_ref[m, rows, :] for m in range(7)]
            mid = x_ref[rows, here]
            up = carry[:, here] if x == 0 else x_ref[(x - 1) * side : x * side, here]
            dn = dn_ref[:, here] * has_dn if x == band - 1 else x_ref[(x + 1) * side : (x + 2) * side, here]
            both = up + dn
            acc = pltpu.roll(rw[0] * both + rw[1] * mid, 1, 0)
            acc = acc + pltpu.roll(rw[2] * both + rw[3] * mid, side - 1, 0)
            acc = acc + (rw[4] * up + rw[5] * dn)
            acc = acc + (rw[6] + cw[6]) * mid
            if not first:
                left = x_ref[rows, pl.ds(pl.multiple_of((j - 1) * side, side), side)]
            if not last:
                right = x_ref[rows, pl.ds(pl.multiple_of((j + 1) * side, side), side)]
            if first:
                both = right
                acc = acc + cw[5] * right
            elif last:
                both = left
                acc = acc + cw[4] * left
            else:
                both = left + right
                acc = acc + (cw[4] * left + cw[5] * right)
            acc = acc + pltpu.roll(cw[0] * both + cw[1] * mid, 1, 1)
            acc = acc + pltpu.roll(cw[2] * both + cw[3] * mid, side - 1, 1)
            if first_stage:
                o_ref[rows, here] = base_ref[rows, here] + acc
            else:
                o_ref[rows, here] = base_ref[rows, here] + (time_step * mid + second_scale * acc)

    block(0, True, False)

    @pl.loop(1, blocks - 1)
    def _(j):
        block(j, False, False)

    block(blocks - 1, False, True)
    carry[...] = x_ref[(band - 1) * side :, :]


def local_stencil(field, base, row_w, col_w, side, first_stage):
    rows, cols = field.shape
    steps = rows // (BAND * side)
    lines = rows // side
    tall = (BAND * side, cols)
    return pl.pallas_call(
        functools.partial(stencil_kernel, side, first_stage),
        grid=(steps,),
        out_shape=jax.ShapeDtypeStruct((rows, cols), jnp.float32),
        in_specs=[
            pl.BlockSpec(tall, lambda i: (i, 0)),
            pl.BlockSpec((side, cols), lambda i: (jnp.minimum(i * BAND + BAND, lines - 1), 0)),
            pl.BlockSpec(tall, lambda i: (i, 0)),
            pl.BlockSpec((7, BAND * side, side), lambda i: (0, i, 0)),
            pl.BlockSpec((8, cols), lambda i: (0, 0)),
        ],
        out_specs=pl.BlockSpec(tall, lambda i: (i, 0)),
        scratch_shapes=[pltpu.VMEM((side, cols), jnp.float32)],
        compiler_params=pltpu.CompilerParams(
            dimension_semantics=("arbitrary",), vmem_limit_bytes=48 * 1024 * 1024
        ),
        cost_estimate=pl.CostEstimate(
            flops=34 * rows * cols, bytes_accessed=14 * rows * cols, transcendentals=0
        ),
    )(field, field, base, row_w, col_w)


def column_weights(cells, row_axis, col_axis):
    nrow, ncol = lax.axis_size(row_axis), lax.axis_size(col_axis)
    if nrow % ncol:
        every = lax.all_gather(cells, row_axis, axis=1, tiled=True)
        count = every.shape[1] // ncol
        return lax.dynamic_slice_in_dim(every, lax.axis_index(col_axis) * count, count, 1)
    ratio = nrow // ncol
    turn = lax.axis_index(row_axis) // ncol
    parts = []
    for e in range(ratio):
        mine = None
        for f in range(ratio):
            perm = [
                ((ratio * c + e) * ncol + d, (f * ncol + d) * ncol + c) for c in range(ncol) for d in range(ncol)
            ]
            got = lax.ppermute(cells, BOTH, perm)
            mine = got if mine is None else mine + got
        parts.append(mine)
    return jnp.concatenate(parts, axis=1)


def pack_kernel(places, above_t, below_t, top, bottom, head, tail, *outs):
    outs[0][...] = above_t[...].T
    outs[1][...] = below_t[...].T
    for piece, out in zip((top, bottom, head, tail), outs[2:]):
        out[...] = piece[...]


def packed(field, side):
    rows, cols = field.shape
    lines, blocks = rows // side, cols // side
    chunk = min(4 * side, rows)
    steps = rows // chunk
    parity = lax.axis_index("row") % 2
    odd = parity == 1
    places = jnp.stack([jnp.where(odd, lines - 1, 2 * lines - 1), jnp.where(odd, 0, lines), parity]).astype(jnp.int32)
    tall, wide = (chunk, side), (side, chunk)
    laid = jax.ShapeDtypeStruct((side, rows), jnp.float32)
    stood = jax.ShapeDtypeStruct((rows, side), jnp.float32)
    return pl.pallas_call(
        pack_kernel,
        grid_spec=pltpu.PrefetchScalarGridSpec(
            num_scalar_prefetch=1,
            grid=(steps,),
            in_specs=[
                pl.BlockSpec(tall, lambda i, p: (i, p[0])),
                pl.BlockSpec(tall, lambda i, p: (i, p[1])),
                pl.BlockSpec(wide, lambda i, p: (0, p[2] * steps + i)),
                pl.BlockSpec(wide, lambda i, p: (lines - 1, p[2] * steps + i)),
                pl.BlockSpec(tall, lambda i, p: (i, 0)),
                pl.BlockSpec(tall, lambda i, p: (i, blocks - 1)),
            ],
            out_specs=[pl.BlockSpec(wide, lambda i, p: (0, i))] * 4 + [pl.BlockSpec(tall, lambda i, p: (i, 0))] * 2,
        ),
        out_shape=[laid] * 4 + [stood] * 2,
        compiler_params=pltpu.CompilerParams(vmem_limit_bytes=40 * 1024 * 1024),
        cost_estimate=pl.CostEstimate(flops=0, bytes_accessed=48 * side * rows, transcendentals=0),
    )(places, *[field] * 6)


def halos_of(field, side):
    nrow, ncol = lax.axis_size("row"), lax.axis_size("col")
    rows, cols = field.shape
    ends, half = nrow - 1, cols // 2
    onward = [(i, i + 1) for i in range(ends)]
    back = [(i + 1, i) for i in range(ends)]
    col_onward = [(i, i + 1) for i in range(ncol - 1)]
    col_back = [(i + 1, i) for i in range(ncol - 1)]
    if nrow != 2 * ncol:
        above = lax.ppermute(field[rows - side :], "row", onward)
        below = lax.ppermute(field[:side], "row", back)
        left = lax.ppermute(field[:, cols - side :], "col", col_onward)
        right = lax.ppermute(field[:, :side], "col", col_back)
        pick = jnp.zeros((1,), jnp.int32)
        return pick, (above[:, :half], above[:, half:], below[:, :half], below[:, half:]), (left, right)

    def flat(r, c):
        return r * ncol + c

    to_below = [(flat(2 * c + r % 2, (r - 1) // 2), flat(r, c)) for r in range(1, nrow) for c in range(ncol)]
    to_above = [(flat(2 * c + r % 2, (r + 1) // 2), flat(r, c)) for r in range(ends) for c in range(ncol)]
    above_t, below_t, top, bottom, head, tail = packed(field, side)
    above = lax.ppermute(bottom, "row", onward)
    below = lax.ppermute(top, "row", back)
    above_t = lax.ppermute(above_t, BOTH, to_below)
    below_t = lax.ppermute(below_t, BOTH, to_above)
    left = lax.ppermute(tail, "col", col_onward)
    right = lax.ppermute(head, "col", col_back)
    pick = (lax.axis_index("row") % 2).astype(jnp.int32).reshape(1)
    return pick, (above_t, above, below_t, below), (left, right)


def col_edge_kernel(side, scale, total_ref, left_ref, right_ref, cw_ref, o_ref):
    start = pl.program_id(0) == 0
    halo = jnp.where(start, left_ref[...], right_ref[...])
    near = jnp.where(start, cw_ref[4:5, :], cw_ref[5:6, :])
    piece = pltpu.roll(cw_ref[0:1, :] * halo, 1, 1) + pltpu.roll(cw_ref[2:3, :] * halo, side - 1, 1) + near * halo
    o_ref[...] = total_ref[...] + scale * piece


def row_edge_kernel(side, scale, pick, total_ref, a_ref, b_ref, c_ref, d_ref, rw_ref, o_ref):
    start = pl.program_id(0) == 0
    picked = pl.program_id(1) // (pl.num_programs(1) // 2) == pick[0]
    near = jnp.where(start, rw_ref[4], rw_ref[5])
    for j in range(total_ref.shape[1] // side):
        here = slice(j * side, (j + 1) * side)
        above = jnp.where(picked, a_ref[:, here], b_ref[:, here])
        below = jnp.where(picked, c_ref[:, here], d_ref[:, here])
        halo = jnp.where(start, above, below)
        piece = pltpu.roll(rw_ref[0] * halo, 1, 0) + pltpu.roll(rw_ref[2] * halo, side - 1, 0) + near * halo
        o_ref[:, here] = total_ref[:, here] + scale * piece


def corrected(total, halos, row_w, col_w, side, scale):
    pick, row_parts, (left, right) = halos
    rows, cols = total.shape
    lines, blocks = rows // side, cols // side
    chunk = min(4 * side, rows)
    same = jax.ShapeDtypeStruct(total.shape, jnp.float32)
    spot = pl.BlockSpec((chunk, side), lambda s, i: (i, s * (blocks - 1)))
    halo = pl.BlockSpec((chunk, side), lambda s, i: (i, 0))
    total = pl.pallas_call(
        functools.partial(col_edge_kernel, side, scale),
        grid=(2, rows // chunk),
        out_shape=same,
        in_specs=[spot, halo, halo, pl.BlockSpec((8, side), lambda s, i: (0, s * (blocks - 1)))],
        out_specs=spot,
        input_output_aliases={0: 0},
        compiler_params=pltpu.CompilerParams(vmem_limit_bytes=40 * 1024 * 1024),
        cost_estimate=pl.CostEstimate(flops=14 * side * rows, bytes_accessed=32 * side * rows, transcendentals=0),
    )(total, left, right, col_w)
    chunk = min(4 * side, cols // 2)
    steps = cols // chunk
    spot = pl.BlockSpec((side, chunk), lambda s, j, p: (s * (lines - 1), j))
    halo = pl.BlockSpec((side, chunk), lambda s, j, p: (0, j % (steps // 2)))
    return pl.pallas_call(
        functools.partial(row_edge_kernel, side, scale),
        grid_spec=pltpu.PrefetchScalarGridSpec(
            num_scalar_prefetch=1,
            grid=(2, steps),
            in_specs=[spot] + [halo] * 4 + [pl.BlockSpec((7, side, side), lambda s, j, p: (0, s * (lines - 1), 0))],
            out_specs=spot,
        ),
        out_shape=same,
        input_output_aliases={1: 0},
        compiler_params=pltpu.CompilerParams(vmem_limit_bytes=40 * 1024 * 1024),
        cost_estimate=pl.CostEstimate(flops=14 * side * cols, bytes_accessed=40 * side * cols, transcendentals=0),
    )(pick, total, *row_parts, row_w)


def per_device(cov, noise, diffusivity, wind_x, wind_y):
    side = diffusivity.shape[1]
    rows, cols = cov.shape
    cells = jnp.stack([diffusivity, wind_x, wind_y])
    row_w = jnp.broadcast_to(term_weights(*cells).reshape(7, rows, 1), (7, rows, side))
    col_w = jnp.pad(term_weights(*column_weights(cells, "row", "col")).reshape(7, cols), ((0, 1), (0, 0)))
    weights = row_w, col_w, side

    halos = halos_of(cov, side)
    first = corrected(local_stencil(cov, noise, *weights, True), halos, *weights, 1.0)
    halos = halos_of(first, side)
    return corrected(local_stencil(first, cov, *weights, False), halos, *weights, second_scale)


def solution(mesh):
    return jax.shard_map(
        per_device,
        mesh=mesh,
        in_specs=(P("row", "col"), P("row", "col"), P("row", None), P("row", None), P("row", None)),
        out_specs=P("row", "col"),
        check_vma=False,
    )
```
